256 devices in a mesh: dp: 64 (over z_hi, y, x), tensor: 4 (over z_lo, core).
Axes of the slice: x: 4, y: 4, z: 8 (z_hi: 4, z_lo: 2; z = z_hi * 2 + z_lo), core: 2. Of those that a mesh axis runs over, the one named last changes fastest.
Arguments:
- queries: bfloat16 [64, 512, 4096], P('dp', 'tensor'), may hold values from -200 to 200
- dialogue_keys: bfloat16 [64, 512, 512], P('dp', 'tensor'), may hold values from -6 to 6
- dialogue_values: bfloat16 [64, 512, 512], P('dp', 'tensor'), may hold values from -6 to 6
- out_grad: bfloat16 [64, 512, 4096], P('dp', 'tensor'), may hold values from -96 to 96
- lengths: int32 [64], P('dp'), may hold values from 128 to 512, as said below
- cartridge: float32 [1024, 2, 512], P('dp', None, 'tensor'), may hold values from -6 to 6
- first_moment: float32 [1024, 2, 512], P('dp', None, 'tensor'), may hold values from -2 to 2
- second_moment: float32 [1024, 2, 512], P('dp', None, 'tensor'), may hold values from 0.01 to 4
Outputs:
- q_grad: bfloat16 [64, 512, 4096], P('dp', 'tensor')
- key_grad: bfloat16 [64, 512, 512], P('dp', 'tensor')
- value_grad: bfloat16 [64, 512, 512], P('dp', 'tensor')
- new_cartridge: float32 [1024, 2, 512], P('dp', None, 'tensor')
- new_m: float32 [1024, 2, 512], P('dp', None, 'tensor')
- new_v: float32 [1024, 2, 512], P('dp', None, 'tensor')
The draws below stay inside these ranges and needn't reach their ends.
Inputs may be any that keep to these rules, and one draw needn't show every extreme that they name: `lengths`: each conversation's real tokens stand at its start; some conversation has exactly 512.
All inputs are finite; a program needn't handle non-finite values.
Results may differ from the reference program's by a relative error of at most 0.0079.
Values may be sent and summed in bfloat16 or wider, within the bound.
No kernel may reach another device: no remote copies, remote signals or barrier semaphores. Data moves between devices by JAX's collectives and lax.ppermute only.
A program may use at most 64 MiB of HBM per device.

```python
import math
import jax
import jax.numpy as jnp
from jax import lax

QUERY_HEADS = 32
KEY_VALUE_HEADS = 4
HEAD_WIDTH = 128
PREFIX_TOKENS = 1024
SLOT_COUNT = 512
STEP = 10
DIALOGUE_COUNT = 64


def shared_keys(key):
    drawn = jax.random.normal(jax.random.fold_in(key, 101), (DIALOGUE_COUNT, SLOT_COUNT, KEY_VALUE_HEADS, HEAD_WIDTH), jnp.float32)
    return jnp.clip(drawn, -6.0, 6.0)


def draw_dialogue_keys(key, part):
    return shared_keys(key).reshape(DIALOGUE_COUNT, SLOT_COUNT, KEY_VALUE_HEADS * HEAD_WIDTH).astype(jnp.bfloat16)


def draw_queries(key, part):
    base = jax.random.normal(jax.random.fold_in(key, 5), (DIALOGUE_COUNT, SLOT_COUNT, QUERY_HEADS * HEAD_WIDTH), jnp.float32)
    return jnp.clip(base, -200.0, 200.0).astype(jnp.bfloat16)


def draw_lengths(key, part):
    drawn = jax.random.randint(key, (DIALOGUE_COUNT,), SLOT_COUNT // 4, SLOT_COUNT + 1)
    longest = jax.random.randint(jax.random.fold_in(key, 11), (), 0, DIALOGUE_COUNT)
    return jnp.where(jnp.arange(DIALOGUE_COUNT) == longest, SLOT_COUNT, drawn).astype(jnp.int32)


def block_levels(key, shape, shards, smallest, high):
    def one(position, parts):
        heights = jax.random.uniform(jax.random.fold_in(jax.random.fold_in(key, 6), position), (parts,), jnp.float32, smallest / len(shards), high / len(shards))
        return jnp.repeat(jnp.exp(heights), shape[position] // parts).reshape((-1,) + (1,) * (len(shape) - position - 1))

    level = one(*shards[0])
    for cut in shards[1:]:
        level = level * one(*cut)
    return level


def scatter_about(rng, extent, width, bound, shards=(), held_as=jnp.bfloat16):
    array = jax.random.normal(rng, extent, jnp.float32) * width
    if len(shards) > 0:
        array = block_levels(rng, extent, shards, -0.22, 0.18) * array
    return jnp.clip(array, min=-bound, max=bound).astype(held_as)


def setup_inputs(seed: int = 0) -> dict:
    keys = jax.random.split(jax.random.key(seed), 9)
    return {
        "queries": draw_queries(jax.random.fold_in(keys[8], 71), 0),
        "dialogue_keys": draw_dialogue_keys(jax.random.fold_in(keys[8], 71), 0),
        "dialogue_values": scatter_about(keys[2], (DIALOGUE_COUNT, SLOT_COUNT, KEY_VALUE_HEADS * HEAD_WIDTH), 1.0, 6.0, ((0, 64), (1, 4))),
        "out_grad": scatter_about(keys[3], (DIALOGUE_COUNT, SLOT_COUNT, QUERY_HEADS * HEAD_WIDTH), 16.0, 96.0, ((0, 64), (1, 4))),
        "lengths": draw_lengths(jax.random.fold_in(keys[8], 71), 0),
        "cartridge": scatter_about(keys[5], (PREFIX_TOKENS, 2, KEY_VALUE_HEADS * HEAD_WIDTH), 1.0, 6.0, ((0, 64), (2, 4)), jnp.float32),
        "first_moment": scatter_about(keys[6], (PREFIX_TOKENS, 2, KEY_VALUE_HEADS * HEAD_WIDTH), 0.3, 2.0, ((0, 64), (2, 4)), jnp.float32),
        "second_moment": jnp.clip(jnp.exp(math.log(4.0) - 5.9914646 * jax.random.uniform(keys[7], (PREFIX_TOKENS, 2, KEY_VALUE_HEADS * HEAD_WIDTH), jnp.float32) ** block_levels(keys[7], (PREFIX_TOKENS, 2, KEY_VALUE_HEADS * HEAD_WIDTH), ((0, 64), (2, 4)), -0.2, 0.2)), 0.01, 4.0),
    }


BETA_ONE = 0.9
BETA_TWO = 0.999
ADAM_EPS = 1e-08
LEARN_RATE = 0.01
MASKED = -1e+30

def head_terms(head_queries, head_grads, all_keys, all_values, score_scale):
    scores = jnp.dot(head_queries, all_keys.T, preferred_element_type=jnp.float32) * score_scale
    key_pos = jnp.arange(all_keys.shape[0]) - PREFIX_TOKENS
    row_pos = jnp.arange(head_queries.shape[0])
    scores = jnp.where(key_pos[None, :] <= row_pos[:, None], scores, MASKED)
    row_max = lax.optimization_barrier(jnp.max(scores, axis=1, keepdims=True))
    exp_scores = jnp.exp(scores - row_max)
    weights = exp_scores / lax.optimization_barrier(jnp.sum(exp_scores, axis=1, keepdims=True))
    weights_half = weights.astype(jnp.bfloat16)
    attended = jnp.dot(weights_half, all_values, preferred_element_type=jnp.float32).astype(jnp.bfloat16)
    row_dot = lax.optimization_barrier(jnp.sum(head_grads.astype(jnp.float32) * attended.astype(jnp.float32), axis=1, keepdims=True))
    weight_grad = jnp.dot(head_grads, all_values.T, preferred_element_type=jnp.float32)
    score_grad = (weights * (weight_grad - row_dot)).astype(jnp.bfloat16)
    query_grad = (jnp.dot(score_grad, all_keys, preferred_element_type=jnp.float32) * score_scale).astype(jnp.bfloat16)
    key_part = jnp.dot(score_grad.T, head_queries, preferred_element_type=jnp.float32) * score_scale
    value_part = jnp.dot(weights_half.T, head_grads, preferred_element_type=jnp.float32)
    return (query_grad, key_part, value_part)

def reference(queries, dialogue_keys, dialogue_values, out_grad, lengths, cartridge, first_moment, second_moment):
    score_scale = HEAD_WIDTH ** (-0.5)
    prefix = cartridge.astype(jnp.bfloat16)
    head_group_size = QUERY_HEADS // KEY_VALUE_HEADS
    positions = jnp.arange(SLOT_COUNT)

    def one_sample(running, inputs):
        sample_queries, sample_keys, sample_values, sample_grads, sample_length = inputs
        sample_grads = jnp.where((positions < sample_length)[:, None], sample_grads, jnp.zeros((), sample_grads.dtype))
        query_parts, key_parts, value_parts, prefix_kparts, prefix_vparts = ([], [], [], [], [])
        for head_group_index in range(KEY_VALUE_HEADS):
            columns = slice(head_group_index * HEAD_WIDTH, (head_group_index + 1) * HEAD_WIDTH)
            all_keys = jnp.concatenate([prefix[:, 0, columns], sample_keys[:, columns]], 0)
            all_values = jnp.concatenate([prefix[:, 1, columns], sample_values[:, columns]], 0)
            head_columns = slice(head_group_index * head_group_size * HEAD_WIDTH, (head_group_index + 1) * head_group_size * HEAD_WIDTH)
            head_queries = sample_queries[:, head_columns].reshape(SLOT_COUNT, head_group_size, HEAD_WIDTH).transpose(1, 0, 2)
            head_grads = sample_grads[:, head_columns].reshape(SLOT_COUNT, head_group_size, HEAD_WIDTH).transpose(1, 0, 2)
            query_grad, key_part, value_part = jax.vmap(head_terms, in_axes=(0, 0, None, None, None))(head_queries, head_grads, all_keys, all_values, score_scale)
            key_part = lax.optimization_barrier(jnp.sum(key_part, 0))
            value_part = lax.optimization_barrier(jnp.sum(value_part, 0))
            query_parts.append(query_grad.transpose(1, 0, 2).reshape(SLOT_COUNT, head_group_size * HEAD_WIDTH))
            key_parts.append(key_part[PREFIX_TOKENS:].astype(jnp.bfloat16))
            value_parts.append(value_part[PREFIX_TOKENS:].astype(jnp.bfloat16))
            prefix_kparts.append(key_part[:PREFIX_TOKENS])
            prefix_vparts.append(value_part[:PREFIX_TOKENS])
        term = jnp.stack([jnp.concatenate(prefix_kparts, 1), jnp.concatenate(prefix_vparts, 1)], 1)
        return (running + term, (jnp.concatenate(query_parts, 1), jnp.concatenate(key_parts, 1), jnp.concatenate(value_parts, 1)))
    initial_sum = jnp.zeros((PREFIX_TOKENS, 2, KEY_VALUE_HEADS * HEAD_WIDTH), jnp.float32)
    prefix_grad, (q_grad, key_grad, value_grad) = lax.scan(one_sample, initial_sum, (queries, dialogue_keys, dialogue_values, out_grad, lengths))
    new_m = BETA_ONE * first_moment + (1.0 - BETA_ONE) * prefix_grad
    new_v = BETA_TWO * second_moment + (1.0 - BETA_TWO) * prefix_grad * prefix_grad
    update = new_m / (1.0 - BETA_ONE ** STEP) / (jnp.sqrt(new_v / (1.0 - BETA_TWO ** STEP)) + ADAM_EPS)
    new_cartridge = cartridge - LEARN_RATE * update
    return (q_grad, key_grad, value_grad, new_cartridge, new_m, new_v)
```

```python
import jax
import jax.numpy as jnp
from jax import lax
from jax.experimental import pallas as pl
from jax.experimental.pallas import tpu as pltpu
from jax.sharding import PartitionSpec as P

QUERY_HEADS = 32
KEY_VALUE_HEADS = 4
HEAD_WIDTH = 128
PREFIX_TOKENS = 1024
SLOT_COUNT = 512
STEP = 10

BETA_ONE = 0.9
BETA_TWO = 0.999
ADAM_EPS = 1e-08
LEARN_RATE = 0.01
MASKED = -1e30
GROUP = QUERY_HEADS // KEY_VALUE_HEADS
ALL_TOKENS = PREFIX_TOKENS + SLOT_COUNT
SCALE = HEAD_WIDTH ** (-0.5)
LOG2_SCALE = SCALE * 1.4426950408889634

ROWS = 256
CHUNK = 256
BLOCKS = SLOT_COUNT // ROWS

bf16 = jnp.bfloat16
f32 = jnp.float32


def nn(a, b):
    return jnp.dot(a, b, preferred_element_type=f32)


def nt(a, b):
    return lax.dot_general(a, b, (((1,), (1,)), ((), ())), preferred_element_type=f32)


def turned(a):
    return a.astype(f32).T


def attention_kernel(
    length_ref, q_ref, g_ref, kv_ref, prefix_ref, qgrad_ref, kvgrad_ref, pgrad_ref,
    keys, values, keys_t, values_t, dkeys, dvalues, exps,
):
    head = pl.program_id(0)
    length = length_ref[0]

    @pl.when(head == 0)
    def _():
        keys[:PREFIX_TOKENS] = prefix_ref[:, :HEAD_WIDTH]
        keys[PREFIX_TOKENS:] = kv_ref[:, :HEAD_WIDTH]
        values[:PREFIX_TOKENS] = prefix_ref[:, HEAD_WIDTH:]
        values[PREFIX_TOKENS:] = kv_ref[:, HEAD_WIDTH:]
        for start in range(0, ALL_TOKENS, CHUNK):
            span = slice(start, start + CHUNK)
            keys_t[:, span] = turned(keys[span]).astype(bf16)
            values_t[:, span] = turned(values[span]).astype(bf16)
        dkeys[...] = jnp.zeros_like(dkeys)
        dvalues[...] = jnp.zeros_like(dvalues)

    for block in range(BLOCKS):
        first = block * ROWS
        rows = slice(first, first + ROWS)
        spans = [slice(s, s + CHUNK) for s in range(0, PREFIX_TOKENS + first + ROWS, CHUNK)]
        q = q_ref[rows]
        row_index = first + lax.broadcasted_iota(jnp.int32, (ROWS, HEAD_WIDTH), 0)
        g = jnp.where(row_index < length, g_ref[rows], jnp.zeros((), bf16))
        g_t = turned(g)
        top = None
        for span in spans:
            scores = nt(keys[span], q)
            if span.stop > PREFIX_TOKENS + first:
                key_pos = span.start - PREFIX_TOKENS + lax.broadcasted_iota(jnp.int32, (CHUNK, ROWS), 0)
                row_pos = first + lax.broadcasted_iota(jnp.int32, (CHUNK, ROWS), 1)
                scores = jnp.where(key_pos <= row_pos, scores, MASKED)
            exps[block, span] = scores
            chunk_top = jnp.max(scores, axis=0, keepdims=True)
            top = chunk_top if top is None else jnp.maximum(top, chunk_top)
        total = jnp.zeros((1, ROWS), f32)
        for span in spans:
            e = jnp.exp2((exps[block, span] - top) * LOG2_SCALE)
            exps[block, span] = e
            total = total + jnp.sum(e, axis=0, keepdims=True)
        inverse = 1.0 / total
        attended_t = jnp.zeros((HEAD_WIDTH, ROWS), f32)
        for span in spans:
            weights = exps[block, span] * inverse
            exps[block, span] = weights
            half = weights.astype(bf16)
            attended_t = attended_t + nn(values_t[:, span], half)
            dvalues[span] += nn(half, g)
        row_dot = jnp.sum(g_t * attended_t.astype(bf16).astype(f32), axis=0, keepdims=True)
        qgrad_t = jnp.zeros((HEAD_WIDTH, ROWS), f32)
        for span in spans:
            weight_grad = nt(values[span], g)
            score_grad = (exps[block, span] * (weight_grad - row_dot)).astype(bf16)
            qgrad_t = qgrad_t + nn(keys_t[:, span], score_grad)
            dkeys[span] += nn(score_grad, q)
        qgrad_ref[rows] = (qgrad_t * SCALE).T.astype(bf16)

    @pl.when(head == GROUP - 1)
    def _():
        pgrad_ref[:, :HEAD_WIDTH] = (dkeys[:PREFIX_TOKENS] * SCALE).astype(bf16)
        pgrad_ref[:, HEAD_WIDTH:] = dvalues[:PREFIX_TOKENS].astype(bf16)
        kvgrad_ref[:, :HEAD_WIDTH] = (dkeys[PREFIX_TOKENS:] * SCALE).astype(bf16)
        kvgrad_ref[:, HEAD_WIDTH:] = dvalues[PREFIX_TOKENS:].astype(bf16)


def attention(length, tokens, prefix):
    return pl.pallas_call(
        attention_kernel,
        grid=(GROUP,),
        in_specs=[
            pl.BlockSpec(memory_space=pltpu.SMEM),
            pl.BlockSpec((SLOT_COUNT, HEAD_WIDTH), lambda h: (0, h)),
            pl.BlockSpec((SLOT_COUNT, HEAD_WIDTH), lambda h: (0, GROUP + h)),
            pl.BlockSpec((SLOT_COUNT, 2 * HEAD_WIDTH), lambda h: (0, GROUP)),
            pl.BlockSpec((PREFIX_TOKENS, 2 * HEAD_WIDTH), lambda h: (0, 0)),
        ],
        out_specs=[
            pl.BlockSpec((SLOT_COUNT, HEAD_WIDTH), lambda h: (0, h)),
            pl.BlockSpec((SLOT_COUNT, 2 * HEAD_WIDTH), lambda h: (0, 0)),
            pl.BlockSpec((PREFIX_TOKENS, 2 * HEAD_WIDTH), lambda h: (0, 0)),
        ],
        out_shape=[
            jax.ShapeDtypeStruct((SLOT_COUNT, GROUP * HEAD_WIDTH), bf16),
            jax.ShapeDtypeStruct((SLOT_COUNT, 2 * HEAD_WIDTH), bf16),
            jax.ShapeDtypeStruct((PREFIX_TOKENS, 2 * HEAD_WIDTH), bf16),
        ],
        scratch_shapes=[
            pltpu.VMEM((ALL_TOKENS, HEAD_WIDTH), bf16),
            pltpu.VMEM((ALL_TOKENS, HEAD_WIDTH), bf16),
            pltpu.VMEM((HEAD_WIDTH, ALL_TOKENS), bf16),
            pltpu.VMEM((HEAD_WIDTH, ALL_TOKENS), bf16),
            pltpu.VMEM((ALL_TOKENS, HEAD_WIDTH), f32),
            pltpu.VMEM((ALL_TOKENS, HEAD_WIDTH), f32),
            pltpu.VMEM((BLOCKS, ALL_TOKENS, ROWS), f32),
        ],
        compiler_params=pltpu.CompilerParams(
            dimension_semantics=("arbitrary",), vmem_limit_bytes=40 * 1024 * 1024
        ),
        cost_estimate=pl.CostEstimate(flops=9 * 10**9, bytes_accessed=5 * 10**6, transcendentals=6 * 10**6),
    )(length, tokens, tokens, tokens, prefix)


def shards(
    queries,
    dialogue_keys,
    dialogue_values,
    out_grad,
    lengths,
    cartridge,
    first_moment,
    second_moment,
):
    tensor_size = lax.axis_size("tensor")
    dp_size = lax.axis_size("dp")
    own_rows = SLOT_COUNT // tensor_size
    head_columns = GROUP * HEAD_WIDTH

    own_prefix = cartridge.astype(bf16).reshape(PREFIX_TOKENS // dp_size, 2 * HEAD_WIDTH)
    prefix = lax.all_to_all(
        jnp.broadcast_to(own_prefix[None], (dp_size,) + own_prefix.shape), "dp", 0, 0
    ).reshape(PREFIX_TOKENS, 2 * HEAD_WIDTH)

    outgoing = jnp.stack(
        [
            jnp.concatenate(
                [
                    queries[0, :, t * head_columns : (t + 1) * head_columns],
                    out_grad[0, :, t * head_columns : (t + 1) * head_columns],
                    dialogue_keys[0, :, t * HEAD_WIDTH : (t + 1) * HEAD_WIDTH],
                    dialogue_values[0, :, t * HEAD_WIDTH : (t + 1) * HEAD_WIDTH],
                ],
                1,
            )
            for t in range(tensor_size)
        ]
    )
    tokens = lax.all_to_all(outgoing, "tensor", 0, 0).reshape(SLOT_COUNT, -1)

    query_grad, kv_grad, prefix_part = attention(lengths, tokens, prefix)

    arrived = lax.all_to_all(
        prefix_part.reshape(dp_size, PREFIX_TOKENS // dp_size, 2 * HEAD_WIDTH), "dp", 0, 0
    )
    returned = lax.all_to_all(
        jnp.concatenate([query_grad, kv_grad], 1).reshape(tensor_size, own_rows, -1), "tensor", 0, 0
    )
    q_grad = jnp.concatenate([returned[t, :, :head_columns] for t in range(tensor_size)], 1)[None]
    key_grad = jnp.concatenate(
        [returned[t, :, head_columns : head_columns + HEAD_WIDTH] for t in range(tensor_size)], 1
    )[None]
    value_grad = jnp.concatenate(
        [returned[t, :, head_columns + HEAD_WIDTH :] for t in range(tensor_size)], 1
    )[None]

    prefix_grad = jnp.sum(arrived.astype(f32), 0).reshape(cartridge.shape)
    new_m = BETA_ONE * first_moment + (1.0 - BETA_ONE) * prefix_grad
    new_v = BETA_TWO * second_moment + (1.0 - BETA_TWO) * prefix_grad * prefix_grad
    update = new_m / (1.0 - BETA_ONE**STEP) / (jnp.sqrt(new_v / (1.0 - BETA_TWO**STEP)) + ADAM_EPS)
    new_cartridge = cartridge - LEARN_RATE * update
    return (q_grad, key_grad, value_grad, new_cartridge, new_m, new_v)


def solution(mesh):
    tokens = P("dp", "tensor", None)
    trained = P("dp", None, "tensor")
    return jax.shard_map(
        shards,
        mesh=mesh,
        in_specs=(tokens, tokens, tokens, tokens, P("dp"), trained, trained, trained),
        out_specs=(tokens, tokens, tokens, trained, trained, trained),
        check_vma=False,
    )
```

```python
import functools

import jax
import jax.numpy as jnp
from jax import lax
from jax.experimental import pallas as pl
from jax.experimental.pallas import tpu as pltpu
from jax.sharding import PartitionSpec as P

QUERY_HEADS = 32
KEY_VALUE_HEADS = 4
HEAD_WIDTH = 128
PREFIX_TOKENS = 1024
SLOT_COUNT = 512
STEP = 10

BETA_ONE = 0.9
BETA_TWO = 0.999
ADAM_EPS = 1e-08
LEARN_RATE = 0.01
MASKED = -1e30
GROUP = QUERY_HEADS // KEY_VALUE_HEADS
ALL_TOKENS = PREFIX_TOKENS + SLOT_COUNT
SCALE = HEAD_WIDTH ** (-0.5)
LOG2_SCALE = SCALE * 1.4426950408889634

PEERS = 4
OWN_ROWS = SLOT_COUNT // PEERS
PLANE = 16
PLANES = 4
SHARE = PREFIX_TOKENS // (PLANE * PLANES)
IN_PLANE = [[z * PLANE + r for r in range(PLANE)] for z in range(PLANES)]

HALVES = 2
HALF_HEADS = GROUP // HALVES
HALF = HALF_HEADS * HEAD_WIDTH
TOGETHER = 2
ROWS = 256
CHUNK = 512
BLOCKS = SLOT_COUNT // ROWS

bf16 = jnp.bfloat16
f32 = jnp.float32
VMEM = pl.BlockSpec(memory_space=pltpu.VMEM)
SMEM = pl.BlockSpec(memory_space=pltpu.SMEM)
PARAMS = pltpu.CompilerParams(vmem_limit_bytes=28 * 1024 * 1024)


def nn(a, b):
    return jnp.dot(a, b, preferred_element_type=f32)


def turned(a):
    return a.astype(f32).T


def part_start(place, peer, width):
    return pl.multiple_of(jnp.bitwise_xor(place, peer) * width, width)


def outgoing_kernel(place_ref, *refs):
    outs, held, sems = refs[4 : 4 + 2 * PEERS], refs[4 + 2 * PEERS : -1], refs[-1]
    copies = [pltpu.make_async_copy(refs[i], held[i], sems.at[i]) for i in range(4)]
    for copy in copies:
        copy.start()
    for copy in copies:
        copy.wait()
    q_ref, g_ref, k_ref, v_ref = held
    place = place_ref[0]
    for peer in range(PEERS):
        heads = part_start(place, peer, GROUP * HEAD_WIDTH)
        shared = pl.ds(part_start(place, peer, HEAD_WIDTH), HEAD_WIDTH)
        for half in range(HALVES):
            out = outs[half * PEERS + peer]
            own = pl.ds(pl.multiple_of(heads + half * HALF, HALF), HALF)
            out[:, :HALF] = q_ref[0, :, own]
            out[:, HALF : 2 * HALF] = g_ref[0, :, own]
        out = outs[peer]
        out[:, 2 * HALF : 2 * HALF + HEAD_WIDTH] = k_ref[0, :, shared]
        out[:, 2 * HALF + HEAD_WIDTH :] = v_ref[0, :, shared]


def outgoing(place, queries, out_grad, dialogue_keys, dialogue_values):
    first = jax.ShapeDtypeStruct((OWN_ROWS, 2 * HALF + 2 * HEAD_WIDTH), bf16)
    second = jax.ShapeDtypeStruct((OWN_ROWS, 2 * HALF), bf16)
    outs = pl.pallas_call(
        outgoing_kernel,
        in_specs=[SMEM] + [pl.BlockSpec(memory_space=pltpu.HBM)] * 4,
        out_specs=[VMEM] * (2 * PEERS),
        out_shape=[first] * PEERS + [second] * PEERS,
        scratch_shapes=[
            pltpu.VMEM(x.shape, bf16) for x in (queries, out_grad, dialogue_keys, dialogue_values)
        ]
        + [pltpu.SemaphoreType.DMA((4,))],
        compiler_params=pltpu.CompilerParams(vmem_limit_bytes=60 * 1024 * 1024),
        cost_estimate=pl.CostEstimate(flops=0, bytes_accessed=5 * 10**6, transcendentals=0),
    )(place, queries, out_grad, dialogue_keys, dialogue_values)
    return outs[:PEERS], outs[PEERS:]


def assemble_kernel(place_ref, *refs):
    first, second = refs[:PEERS], refs[PEERS : 2 * PEERS]
    q_ref, k_ref, v_ref = refs[2 * PEERS :]
    place = place_ref[0]
    for peer in range(PEERS):
        heads = part_start(place, peer, GROUP * HEAD_WIDTH)
        shared = pl.ds(part_start(place, peer, HEAD_WIDTH), HEAD_WIDTH)
        q_ref[0, :, pl.ds(heads, HALF)] = first[peer][...]
        q_ref[0, :, pl.ds(pl.multiple_of(heads + HALF, HALF), HALF)] = second[peer][:, :HALF]
        k_ref[0, :, shared] = second[peer][:, HALF : HALF + HEAD_WIDTH]
        v_ref[0, :, shared] = second[peer][:, HALF + HEAD_WIDTH :]


def assemble(place, first, second):
    narrow = jax.ShapeDtypeStruct((1, OWN_ROWS, KEY_VALUE_HEADS * HEAD_WIDTH), bf16)
    return pl.pallas_call(
        assemble_kernel,
        in_specs=[SMEM] + [VMEM] * (2 * PEERS),
        out_specs=[VMEM] * 3,
        out_shape=[jax.ShapeDtypeStruct((1, OWN_ROWS, QUERY_HEADS * HEAD_WIDTH), bf16), narrow, narrow],
        compiler_params=PARAMS,
        cost_estimate=pl.CostEstimate(flops=0, bytes_accessed=3 * 10**6, transcendentals=0),
    )(place, *first, *second)


class Unit:
    def __init__(self, slot, head, block):
        self.slot, self.head = slot, head
        self.first = block * ROWS
        self.rows = slice(self.first, self.first + ROWS)
        end = PREFIX_TOKENS + self.first + ROWS
        self.spans = [slice(s, min(s + CHUNK, end)) for s in range(0, end, CHUNK)]
        self.tops, self.top, self.total = [], None, None


def attention_kernel(last, length_ref, place_ref, *refs):
    tokens, shared = refs[:PEERS], refs[PEERS : 2 * PEERS]
    refs = refs[2 * PEERS :]
    prefix_refs, refs = refs[:PLANES], refs[PLANES:]
    if last:
        (dkeys_in, dvalues_in), refs = refs[:2], refs[2:]
    outs, refs = refs[:PEERS], refs[PEERS:]
    (dkeys_out, dvalues_out) = (None, None) if last else refs[:2]
    pgrad_ref = refs[0] if last else None
    refs = refs[1:] if last else refs[2:]
    keys, values, keys_t, values_t, dkeys, dvalues, exps, q_all, g_all, qgrad_all = refs
    if not last:
        dkeys, dvalues = dkeys_out, dvalues_out
    length, place = length_ref[0], place_ref[0]

    for k in range(PLANES):
        plane = slice(k * PLANE * SHARE, (k + 1) * PLANE * SHARE)
        keys[plane] = prefix_refs[k][:, :HEAD_WIDTH]
        values[plane] = prefix_refs[k][:, HEAD_WIDTH:]
    for peer in range(PEERS):
        rows = pl.ds(part_start(place, peer, OWN_ROWS), OWN_ROWS)
        there = pl.ds(pl.multiple_of(PREFIX_TOKENS + part_start(place, peer, OWN_ROWS), OWN_ROWS), OWN_ROWS)
        keys[there] = shared[peer][:, 2 * HALF : 2 * HALF + HEAD_WIDTH]
        values[there] = shared[peer][:, 2 * HALF + HEAD_WIDTH :]
        q_all[rows] = tokens[peer][:, :HALF]
        g_all[rows] = tokens[peer][:, HALF : 2 * HALF]
    for start in range(0, ALL_TOKENS, 256):
        span = slice(start, start + 256)
        keys_t[:, span] = turned(keys[span]).astype(bf16)
        values_t[:, span] = turned(values[span]).astype(bf16)
    dkeys[...] = jnp.zeros_like(dkeys)
    dvalues[...] = jnp.zeros_like(dvalues)

    def prepare(u):
        q = q_all[u.rows, u.head]
        row_index = u.first + lax.broadcasted_iota(jnp.int32, (ROWS, HEAD_WIDTH), 0)
        u.q = q
        u.g = jnp.where(row_index < length, g_all[u.rows, u.head], jnp.zeros((), bf16))
        u.q_t = turned(q).astype(bf16)
        u.g_wide = turned(u.g)
        u.g_t = u.g_wide.astype(bf16)

    def forward(u, i):
        span = u.spans[i]
        scores = nn(keys[span], u.q_t)
        masked = PREFIX_TOKENS + u.first
        if span.stop > masked:
            skip = max(span.start, masked) - span.start
            shape = (span.stop - span.start - skip, ROWS)
            key_pos = span.start + skip - PREFIX_TOKENS + lax.broadcasted_iota(jnp.int32, shape, 0)
            row_pos = u.first + lax.broadcasted_iota(jnp.int32, shape, 1)
            tail = jnp.where(key_pos <= row_pos, scores[skip:], MASKED)
            scores = jnp.concatenate([scores[:skip], tail], 0) if skip else tail
        top = jnp.max(scores, axis=0, keepdims=True)
        top = top if u.top is None else jnp.maximum(top, u.top)
        e = jnp.exp2((scores - top) * LOG2_SCALE)
        exps[u.slot, span] = e
        total = jnp.sum(e, axis=0, keepdims=True)
        u.total = total if u.top is None else u.total * jnp.exp2((u.top - top) * LOG2_SCALE) + total
        u.top = top
        u.tops.append(top)

    def end_forward(u):
        inverse = 1.0 / u.total
        u.factors = [jnp.exp2((top - u.top) * LOG2_SCALE) * inverse for top in u.tops]
        u.attended = jnp.zeros((HEAD_WIDTH, ROWS), f32)
        u.qgrad = jnp.zeros((HEAD_WIDTH, ROWS), f32)

    def attend(u, i):
        span = u.spans[i]
        half = (exps[u.slot, span] * u.factors[i]).astype(bf16)
        u.attended = u.attended + nn(values_t[:, span], half)
        dvalues[span] += nn(half, u.g)

    def end_attend(u):
        u.row_dot = jnp.sum(u.g_wide * u.attended.astype(bf16).astype(f32), axis=0, keepdims=True)

    def backward(u, i):
        span = u.spans[i]
        weight_grad = nn(values[span], u.g_t)
        score_grad = (exps[u.slot, span] * u.factors[i] * (weight_grad - u.row_dot)).astype(bf16)
        u.qgrad = u.qgrad + nn(keys_t[:, span], score_grad)
        dkeys[span] += nn(score_grad, u.q)

    def end_backward(u):
        qgrad_all[u.rows, u.head] = (u.qgrad * SCALE).T.astype(bf16)

    def some_heads(step, carry):
        units = []
        for h in range(TOGETHER):
            start = pl.multiple_of((step * TOGETHER + h) * HEAD_WIDTH, HEAD_WIDTH)
            for block in range(BLOCKS):
                units.append(Unit(len(units), pl.ds(start, HEAD_WIDTH), block))
        for u in units:
            prepare(u)
        stages = ((forward, end_forward), (attend, end_attend), (backward, end_backward))
        for t in range(len(units) + len(stages) - 1):
            live = [(units[t - s], *stages[s]) for s in range(len(stages)) if 0 <= t - s < len(units)]
            for i in range(max(len(u.spans) for u, _, _ in live)):
                for u, work, _ in live:
                    if i < len(u.spans):
                        work(u, i)
            for u, _, end in live:
                end(u)
        return carry

    lax.fori_loop(0, HALF_HEADS // TOGETHER, some_heads, 0)

    for peer in range(PEERS):
        rows = pl.ds(part_start(place, peer, OWN_ROWS), OWN_ROWS)
        outs[peer][:, :HALF] = qgrad_all[rows]
        if last:
            there = pl.ds(pl.multiple_of(PREFIX_TOKENS + part_start(place, peer, OWN_ROWS), OWN_ROWS), OWN_ROWS)
            outs[peer][:, HALF : HALF + HEAD_WIDTH] = ((dkeys[there] + dkeys_in[there]) * SCALE).astype(bf16)
            outs[peer][:, HALF + HEAD_WIDTH :] = (dvalues[there] + dvalues_in[there]).astype(bf16)
    if last:
        for k in range(PLANE * PLANES):
            rows = slice(k * SHARE, (k + 1) * SHARE)
            there = jnp.bitwise_xor(place_ref[1], (k // PLANES % 4) * 4 + k // PLANE), k % PLANES
            pgrad_ref[there[0], there[1], :, :HEAD_WIDTH] = ((dkeys[rows] + dkeys_in[rows]) * SCALE).astype(bf16)
            pgrad_ref[there[0], there[1], :, HEAD_WIDTH:] = (dvalues[rows] + dvalues_in[rows]).astype(bf16)


def attention(length, place, tokens, shared, prefix, sums=None):
    last = sums is not None
    out = jax.ShapeDtypeStruct((OWN_ROWS, HALF + (2 * HEAD_WIDTH if last else 0)), bf16)
    running = jax.ShapeDtypeStruct((ALL_TOKENS, HEAD_WIDTH), f32)
    outs = [out] * PEERS
    outs += [jax.ShapeDtypeStruct((PLANE, PLANES, SHARE, 2 * HEAD_WIDTH), bf16)] if last else [running] * 2
    operands = (*tokens, *shared, *prefix, *(sums or ()))
    half = pltpu.VMEM((ALL_TOKENS, HEAD_WIDTH), bf16)
    half_t = pltpu.VMEM((HEAD_WIDTH, ALL_TOKENS), bf16)
    wide = pltpu.VMEM((ALL_TOKENS, HEAD_WIDTH), f32)
    every = pltpu.VMEM((SLOT_COUNT, HALF), bf16)
    small = pltpu.VMEM((8, HEAD_WIDTH), f32)
    total = wide if last else small
    return pl.pallas_call(
        functools.partial(attention_kernel, last),
        in_specs=[SMEM] * 2 + [VMEM] * len(operands),
        out_specs=[VMEM] * len(outs),
        out_shape=outs,
        scratch_shapes=[
            half, half, half_t, half_t, total, total,
            pltpu.VMEM((TOGETHER * BLOCKS, ALL_TOKENS, ROWS), f32),
            every, every, every,
        ],
        compiler_params=PARAMS,
        cost_estimate=pl.CostEstimate(flops=5 * 10**9, bytes_accessed=5 * 10**6, transcendentals=3 * 10**6),
    )(length, place, *operands)


def shards(
    queries,
    dialogue_keys,
    dialogue_values,
    out_grad,
    lengths,
    cartridge,
    first_moment,
    second_moment,
):
    place = jnp.stack([lax.axis_index("tensor"), lax.axis_index("dp") % PLANE])

    def exchange(parts):
        return [
            lax.ppermute(part, "tensor", [(i, i ^ peer) for i in range(PEERS)]) if peer else part
            for peer, part in enumerate(parts)
        ]

    def across(parts, stride=PLANE):
        size = PLANE * PLANES
        return [
            lax.ppermute(part, "dp", [(i, i ^ (k * stride)) for i in range(size)]) if k else part
            for k, part in enumerate(parts)
        ]

    own_prefix = cartridge.astype(bf16).reshape(SHARE, 2 * HEAD_WIDTH)
    column = across([own_prefix] * 4)
    first, second = outgoing(place, queries, out_grad, dialogue_keys, dialogue_values)
    column, own_part = lax.optimization_barrier((column, first[0]))
    first = [own_part, *first[1:]]
    column = jnp.concatenate(column)
    plane = jnp.concatenate(across([column] * 4, 4))
    prefix = across([plane] * 4, 1)
    first = exchange(first)
    first, second = lax.optimization_barrier((first, second))
    second = exchange(second)

    *first_grad, key_sum, value_sum = attention(lengths, place, first, first, prefix)
    first_back = exchange(first_grad)
    *second_grad, prefix_part = attention(lengths, place, second, first, prefix, (key_sum, value_sum))

    arrived = lax.all_to_all(prefix_part, "dp", 0, 0, axis_index_groups=IN_PLANE)
    second_back = exchange(second_grad)
    plane_sum = jnp.sum(arrived.astype(f32), 0).astype(bf16)
    arrived = across([plane_sum[k] for k in range(PLANES)])
    prefix_grad = sum(part.astype(f32) for part in arrived).reshape(cartridge.shape)
    q_grad, key_grad, value_grad = assemble(place, first_back, second_back)

    new_m = BETA_ONE * first_moment + (1.0 - BETA_ONE) * prefix_grad
    new_v = BETA_TWO * second_moment + (1.0 - BETA_TWO) * prefix_grad * prefix_grad
    update = new_m / (1.0 - BETA_ONE**STEP) / (jnp.sqrt(new_v / (1.0 - BETA_TWO**STEP)) + ADAM_EPS)
    new_cartridge = cartridge - LEARN_RATE * update
    return (q_grad, key_grad, value_grad, new_cartridge, new_m, new_v)


def solution(mesh):
    tokens = P("dp", "tensor", None)
    trained = P("dp", None, "tensor")
    return jax.shard_map(
        shards,
        mesh=mesh,
        in_specs=(tokens, tokens, tokens, tokens, P("dp"), trained, trained, trained),
        out_specs=(tokens, tokens, tokens, trained, trained, trained),
        check_vma=False,
    )
```

```python
import functools

import jax
import jax.numpy as jnp
from jax import lax
from jax.experimental import pallas as pl
from jax.experimental.pallas import tpu as pltpu
from jax.sharding import PartitionSpec as P

QUERY_HEADS = 32
KEY_VALUE_HEADS = 4
HEAD_WIDTH = 128
PREFIX_TOKENS = 1024
SLOT_COUNT = 512
STEP = 10

BETA_ONE = 0.9
BETA_TWO = 0.999
ADAM_EPS = 1e-08
LEARN_RATE = 0.01
MASKED = -1e30
GROUP = QUERY_HEADS // KEY_VALUE_HEADS
ALL_TOKENS = PREFIX_TOKENS + SLOT_COUNT
SCALE = HEAD_WIDTH ** (-0.5)
LOG2_SCALE = SCALE * 1.4426950408889634

PEERS = 4
OWN_ROWS = SLOT_COUNT // PEERS
PLANE = 16
PLANES = 4
SHARE = PREFIX_TOKENS // (PLANE * PLANES)
IN_PLANE = [[z * PLANE + r for r in range(PLANE)] for z in range(PLANES)]

HALVES = 2
HALF_HEADS = GROUP // HALVES
HALF = HALF_HEADS * HEAD_WIDTH
ROWS = 256
CHUNK = 1024
WIDE = HALF_HEADS * ROWS
BLOCKS = SLOT_COUNT // ROWS

bf16 = jnp.bfloat16
f32 = jnp.float32
VMEM = pl.BlockSpec(memory_space=pltpu.VMEM)
SMEM = pl.BlockSpec(memory_space=pltpu.SMEM)
PARAMS = pltpu.CompilerParams(vmem_limit_bytes=36 * 1024 * 1024)


def nn(a, b):
    return jnp.dot(a, b, preferred_element_type=f32)


def turned(a):
    return a.astype(f32).T


def part_start(place, peer, width):
    return pl.multiple_of(jnp.bitwise_xor(place, peer) * width, width)


def outgoing_kernel(place_ref, *refs):
    outs, held, sems = refs[4 : 4 + 2 * PEERS], refs[4 + 2 * PEERS : -1], refs[-1]
    copies = [pltpu.make_async_copy(refs[i], held[i], sems.at[i]) for i in range(4)]
    for copy in copies:
        copy.start()
    for copy in copies:
        copy.wait()
    q_ref, g_ref, k_ref, v_ref = held
    place = place_ref[0]
    for peer in range(PEERS):
        heads = part_start(place, peer, GROUP * HEAD_WIDTH)
        shared = pl.ds(part_start(place, peer, HEAD_WIDTH), HEAD_WIDTH)
        for half in range(HALVES):
            out = outs[half * PEERS + peer]
            own = pl.ds(pl.multiple_of(heads + half * HALF, HALF), HALF)
            out[:, :HALF] = q_ref[0, :, own]
            out[:, HALF : 2 * HALF] = g_ref[0, :, own]
        out = outs[peer]
        out[:, 2 * HALF : 2 * HALF + HEAD_WIDTH] = k_ref[0, :, shared]
        out[:, 2 * HALF + HEAD_WIDTH :] = v_ref[0, :, shared]


def outgoing(place, queries, out_grad, dialogue_keys, dialogue_values):
    first = jax.ShapeDtypeStruct((OWN_ROWS, 2 * HALF + 2 * HEAD_WIDTH), bf16)
    second = jax.ShapeDtypeStruct((OWN_ROWS, 2 * HALF), bf16)
    outs = pl.pallas_call(
        outgoing_kernel,
        in_specs=[SMEM] + [pl.BlockSpec(memory_space=pltpu.HBM)] * 4,
        out_specs=[VMEM] * (2 * PEERS),
        out_shape=[first] * PEERS + [second] * PEERS,
        scratch_shapes=[
            pltpu.VMEM(x.shape, bf16) for x in (queries, out_grad, dialogue_keys, dialogue_values)
        ]
        + [pltpu.SemaphoreType.DMA((4,))],
        compiler_params=pltpu.CompilerParams(vmem_limit_bytes=60 * 1024 * 1024),
        cost_estimate=pl.CostEstimate(flops=0, bytes_accessed=5 * 10**6, transcendentals=0),
    )(place, queries, out_grad, dialogue_keys, dialogue_values)
    return outs[:PEERS], outs[PEERS:]


def assemble_kernel(place_ref, *refs):
    first, second = refs[:PEERS], refs[PEERS : 2 * PEERS]
    q_ref, k_ref, v_ref = refs[2 * PEERS :]
    place = place_ref[0]
    for peer in range(PEERS):
        heads = part_start(place, peer, GROUP * HEAD_WIDTH)
        shared = pl.ds(part_start(place, peer, HEAD_WIDTH), HEAD_WIDTH)
        q_ref[0, :, pl.ds(heads, HALF)] = first[peer][...]
        q_ref[0, :, pl.ds(pl.multiple_of(heads + HALF, HALF), HALF)] = second[peer][:, :HALF]
        k_ref[0, :, shared] = second[peer][:, HALF : HALF + HEAD_WIDTH]
        v_ref[0, :, shared] = second[peer][:, HALF + HEAD_WIDTH :]


def assemble(place, first, second):
    narrow = jax.ShapeDtypeStruct((1, OWN_ROWS, KEY_VALUE_HEADS * HEAD_WIDTH), bf16)
    return pl.pallas_call(
        assemble_kernel,
        in_specs=[SMEM] + [VMEM] * (2 * PEERS),
        out_specs=[VMEM] * 3,
        out_shape=[jax.ShapeDtypeStruct((1, OWN_ROWS, QUERY_HEADS * HEAD_WIDTH), bf16), narrow, narrow],
        compiler_params=PARAMS,
        cost_estimate=pl.CostEstimate(flops=0, bytes_accessed=3 * 10**6, transcendentals=0),
    )(place, *first, *second)


class Unit:
    def __init__(self, slot):
        self.slot = slot
        self.first = slot * ROWS
        self.rows = slice(self.first, self.first + ROWS)
        end = PREFIX_TOKENS + self.first + ROWS
        self.spans = [slice(s, min(s + CHUNK, end)) for s in range(0, end, CHUNK)]
        self.tops, self.top, self.total = [], None, None


def head_columns(head):
    return slice(head * HEAD_WIDTH, (head + 1) * HEAD_WIDTH)


def attention_kernel(last, length_ref, place_ref, *refs):
    tokens, shared = refs[:PEERS], refs[PEERS : 2 * PEERS]
    refs = refs[2 * PEERS :]
    prefix_refs, refs = refs[:PLANES], refs[PLANES:]
    if last:
        (dkeys_in, dvalues_in), refs = refs[:2], refs[2:]
    outs, refs = refs[:PEERS], refs[PEERS:]
    (dkeys_out, dvalues_out) = (None, None) if last else refs[:2]
    pgrad_ref = refs[0] if last else None
    refs = refs[1:] if last else refs[2:]
    keys, values, keys_t, values_t, dkeys, dvalues, exps, q_all, g_all, qgrad_all = refs
    if not last:
        dkeys, dvalues = dkeys_out, dvalues_out
    length, place = length_ref[0], place_ref[0]

    for k in range(PLANES):
        plane = slice(k * PLANE * SHARE, (k + 1) * PLANE * SHARE)
        keys[plane] = prefix_refs[k][:, :HEAD_WIDTH]
        values[plane] = prefix_refs[k][:, HEAD_WIDTH:]
    for peer in range(PEERS):
        rows = pl.ds(part_start(place, peer, OWN_ROWS), OWN_ROWS)
        there = pl.ds(pl.multiple_of(PREFIX_TOKENS + part_start(place, peer, OWN_ROWS), OWN_ROWS), OWN_ROWS)
        keys[there] = shared[peer][:, 2 * HALF : 2 * HALF + HEAD_WIDTH]
        values[there] = shared[peer][:, 2 * HALF + HEAD_WIDTH :]
        q_all[rows] = tokens[peer][:, :HALF]
        g_all[rows] = tokens[peer][:, HALF : 2 * HALF]
    for start in range(0, ALL_TOKENS, 256):
        span = slice(start, start + 256)
        keys_t[:, span] = turned(keys[span]).astype(bf16)
        values_t[:, span] = turned(values[span]).astype(bf16)
    dkeys[...] = jnp.zeros_like(dkeys)
    dvalues[...] = jnp.zeros_like(dvalues)

    def prepare(u):
        row_index = u.first + lax.broadcasted_iota(jnp.int32, (ROWS, HEAD_WIDTH), 0)
        zero = jnp.zeros((), bf16)
        heads = [head_columns(h) for h in range(HALF_HEADS)]
        u.q = jnp.concatenate([q_all[u.rows, h] for h in heads], 0)
        u.g = jnp.concatenate([jnp.where(row_index < length, g_all[u.rows, h], zero) for h in heads], 0)
        u.q_t = turned(u.q).astype(bf16)
        u.g_wide = turned(u.g)
        u.g_t = u.g_wide.astype(bf16)

    def forward(u, i):
        span = u.spans[i]
        scores = nn(keys[span], u.q_t)
        masked = PREFIX_TOKENS + u.first
        if span.stop > masked:
            skip = max(span.start, masked) - span.start
            shape = (span.stop - span.start - skip, WIDE)
            key_pos = span.start + skip - PREFIX_TOKENS + lax.broadcasted_iota(jnp.int32, shape, 0)
            row_pos = u.first + jnp.bitwise_and(lax.broadcasted_iota(jnp.int32, shape, 1), ROWS - 1)
            tail = jnp.where(key_pos <= row_pos, scores[skip:], MASKED)
            scores = jnp.concatenate([scores[:skip], tail], 0) if skip else tail
        top = jnp.max(scores, axis=0, keepdims=True)
        top = top if u.top is None else jnp.maximum(top, u.top)
        e = jnp.exp2((scores - top) * LOG2_SCALE)
        exps[u.slot, span] = e
        total = jnp.sum(e, axis=0, keepdims=True)
        u.total = total if u.top is None else u.total * jnp.exp2((u.top - top) * LOG2_SCALE) + total
        u.top = top
        u.tops.append(top)

    def end_forward(u):
        inverse = 1.0 / u.total
        u.factors = [jnp.exp2((top - u.top) * LOG2_SCALE) * inverse for top in u.tops]
        u.attended = jnp.zeros((HEAD_WIDTH, WIDE), f32)
        u.qgrad = jnp.zeros((HEAD_WIDTH, WIDE), f32)

    def attend(u, i):
        span = u.spans[i]
        half = (exps[u.slot, span] * u.factors[i]).astype(bf16)
        u.attended = u.attended + nn(values_t[:, span], half)
        dvalues[span] += nn(half, u.g)

    def end_attend(u):
        u.row_dot = jnp.sum(u.g_wide * u.attended.astype(bf16).astype(f32), axis=0, keepdims=True)

    def backward(u, i):
        span = u.spans[i]
        weight_grad = nn(values[span], u.g_t)
        score_grad = (exps[u.slot, span] * u.factors[i] * (weight_grad - u.row_dot)).astype(bf16)
        u.qgrad = u.qgrad + nn(keys_t[:, span], score_grad)
        dkeys[span] += nn(score_grad, u.q)

    def end_backward(u):
        turned_back = (u.qgrad * SCALE).T.astype(bf16)
        for h in range(HALF_HEADS):
            qgrad_all[u.rows, head_columns(h)] = turned_back[h * ROWS : (h + 1) * ROWS]

    units = [Unit(slot) for slot in range(BLOCKS)]
    for u in units:
        prepare(u)
    stages = ((forward, end_forward), (attend, end_attend), (backward, end_backward))
    for t in range(len(units) + len(stages) - 1):
        live = [(units[t - s], *stages[s]) for s in range(len(stages)) if 0 <= t - s < len(units)]
        for i in range(max(len(u.spans) for u, _, _ in live)):
            for u, work, _ in live:
                if i < len(u.spans):
                    work(u, i)
        for u, _, end in live:
            end(u)

    for peer in range(PEERS):
        rows = pl.ds(part_start(place, peer, OWN_ROWS), OWN_ROWS)
        outs[peer][:, :HALF] = qgrad_all[rows]
        if last:
            there = pl.ds(pl.multiple_of(PREFIX_TOKENS + part_start(place, peer, OWN_ROWS), OWN_ROWS), OWN_ROWS)
            outs[peer][:, HALF : HALF + HEAD_WIDTH] = ((dkeys[there] + dkeys_in[there]) * SCALE).astype(bf16)
            outs[peer][:, HALF + HEAD_WIDTH :] = (dvalues[there] + dvalues_in[there]).astype(bf16)
    if last:
        for k in range(PLANE * PLANES):
            rows = slice(k * SHARE, (k + 1) * SHARE)
            there = jnp.bitwise_xor(place_ref[1], (k // PLANES % 4) * 4 + k // PLANE), k % PLANES
            pgrad_ref[there[0], there[1], :, :HEAD_WIDTH] = ((dkeys[rows] + dkeys_in[rows]) * SCALE).astype(bf16)
            pgrad_ref[there[0], there[1], :, HEAD_WIDTH:] = (dvalues[rows] + dvalues_in[rows]).astype(bf16)


def attention(length, place, tokens, shared, prefix, sums=None):
    last = sums is not None
    out = jax.ShapeDtypeStruct((OWN_ROWS, HALF + (2 * HEAD_WIDTH if last else 0)), bf16)
    running = jax.ShapeDtypeStruct((ALL_TOKENS, HEAD_WIDTH), f32)
    outs = [out] * PEERS
    outs += [jax.ShapeDtypeStruct((PLANE, PLANES, SHARE, 2 * HEAD_WIDTH), bf16)] if last else [running] * 2
    operands = (*tokens, *shared, *prefix, *(sums or ()))
    half = pltpu.VMEM((ALL_TOKENS, HEAD_WIDTH), bf16)
    half_t = pltpu.VMEM((HEAD_WIDTH, ALL_TOKENS), bf16)
    wide = pltpu.VMEM((ALL_TOKENS, HEAD_WIDTH), f32)
    every = pltpu.VMEM((SLOT_COUNT, HALF), bf16)
    small = pltpu.VMEM((8, HEAD_WIDTH), f32)
    total = wide if last else small
    return pl.pallas_call(
        functools.partial(attention_kernel, last),
        in_specs=[SMEM] * 2 + [VMEM] * len(operands),
        out_specs=[VMEM] * len(outs),
        out_shape=outs,
        scratch_shapes=[
            half, half, half_t, half_t, total, total,
            pltpu.VMEM((BLOCKS, ALL_TOKENS, WIDE), f32),
            every, every, every,
        ],
        compiler_params=PARAMS,
        cost_estimate=pl.CostEstimate(flops=5 * 10**9, bytes_accessed=5 * 10**6, transcendentals=3 * 10**6),
    )(length, place, *operands)


def shards(
    queries,
    dialogue_keys,
    dialogue_values,
    out_grad,
    lengths,
    cartridge,
    first_moment,
    second_moment,
):
    place = jnp.stack([lax.axis_index("tensor"), lax.axis_index("dp") % PLANE])

    def exchange(parts):
        return [
            lax.ppermute(part, "tensor", [(i, i ^ peer) for i in range(PEERS)]) if peer else part
            for peer, part in enumerate(parts)
        ]

    def across(parts, stride=PLANE):
        size = PLANE * PLANES
        return [
            lax.ppermute(part, "dp", [(i, i ^ (k * stride)) for i in range(size)]) if k else part
            for k, part in enumerate(parts)
        ]

    own_prefix = cartridge.astype(bf16).reshape(SHARE, 2 * HEAD_WIDTH)
    column = across([own_prefix] * 4)
    first, second = outgoing(place, queries, out_grad, dialogue_keys, dialogue_values)
    column, own_part = lax.optimization_barrier((column, first[0]))
    first = [own_part, *first[1:]]
    column = jnp.concatenate(column)
    plane = jnp.concatenate(across([column] * 4, 4))
    prefix = across([plane] * 4, 1)
    first = exchange(first)
    first, second = lax.optimization_barrier((first, second))
    second = exchange(second)

    *first_grad, key_sum, value_sum = attention(lengths, place, first, first, prefix)
    first_back = exchange(first_grad)
    *second_grad, prefix_part = attention(lengths, place, second, first, prefix, (key_sum, value_sum))

    arrived = lax.all_to_all(prefix_part, "dp", 0, 0, axis_index_groups=IN_PLANE)
    second_back = exchange(second_grad)
    plane_sum = jnp.sum(arrived.astype(f32), 0).astype(bf16)
    arrived = across([plane_sum[k] for k in range(PLANES)])
    prefix_grad = sum(part.astype(f32) for part in arrived).reshape(cartridge.shape)
    q_grad, key_grad, value_grad = assemble(place, first_back, second_back)

    new_m = BETA_ONE * first_moment + (1.0 - BETA_ONE) * prefix_grad
    new_v = BETA_TWO * second_moment + (1.0 - BETA_TWO) * prefix_grad * prefix_grad
    update = new_m / (1.0 - BETA_ONE**STEP) / (jnp.sqrt(new_v / (1.0 - BETA_TWO**STEP)) + ADAM_EPS)
    new_cartridge = cartridge - LEARN_RATE * update
    return (q_grad, key_grad, value_grad, new_cartridge, new_m, new_v)


def solution(mesh):
    tokens = P("dp", "tensor", None)
    trained = P("dp", None, "tensor")
    return jax.shard_map(
        shards,
        mesh=mesh,
        in_specs=(tokens, tokens, tokens, tokens, P("dp"), trained, trained, trained),
        out_specs=(tokens, tokens, tokens, trained, trained, trained),
        check_vma=False,
    )
```

```python
import functools

import jax
import jax.numpy as jnp
from jax import lax
from jax.experimental import pallas as pl
from jax.experimental.pallas import tpu as pltpu
from jax.sharding import PartitionSpec as P

QUERY_HEADS = 32
KEY_VALUE_HEADS = 4
HEAD_WIDTH = 128
PREFIX_TOKENS = 1024
SLOT_COUNT = 512
STEP = 10

BETA_ONE = 0.9
BETA_TWO = 0.999
ADAM_EPS = 1e-08
LEARN_RATE = 0.01
MASKED = -1e30
GROUP = QUERY_HEADS // KEY_VALUE_HEADS
ALL_TOKENS = PREFIX_TOKENS + SLOT_COUNT
SCALE = HEAD_WIDTH ** (-0.5)
LOG2_SCALE = SCALE * 1.4426950408889634

PEERS = 4
OWN_ROWS = SLOT_COUNT // PEERS
PLANE = 16
PLANES = 4
SHARE = PREFIX_TOKENS // (PLANE * PLANES)
IN_PLANE = [[z * PLANE + r for r in range(PLANE)] for z in range(PLANES)]

HALVES = 2
HALF_HEADS = GROUP // HALVES
HALF = HALF_HEADS * HEAD_WIDTH
ROWS = 256
CHUNK = 1024
WIDE = HALF_HEADS * ROWS
BLOCKS = SLOT_COUNT // ROWS

bf16 = jnp.bfloat16
f32 = jnp.float32
VMEM = pl.BlockSpec(memory_space=pltpu.VMEM)
SMEM = pl.BlockSpec(memory_space=pltpu.SMEM)
PARAMS = pltpu.CompilerParams(vmem_limit_bytes=36 * 1024 * 1024)


def nn(a, b):
    return jnp.dot(a, b, preferred_element_type=f32)


def turned(a):
    return a.astype(f32).T


def part_start(place, peer, width):
    return pl.multiple_of(jnp.bitwise_xor(place, peer) * width, width)


def outgoing_kernel(place_ref, *refs):
    outs, held, sems = refs[4 : 4 + 2 * PEERS], refs[4 + 2 * PEERS : -1], refs[-1]
    copies = [pltpu.make_async_copy(refs[i], held[i], sems.at[i]) for i in range(4)]
    for copy in copies:
        copy.start()
    for copy in copies:
        copy.wait()
    q_ref, g_ref, k_ref, v_ref = held
    place = place_ref[0]
    for peer in range(PEERS):
        heads = part_start(place, peer, GROUP * HEAD_WIDTH)
        shared = pl.ds(part_start(place, peer, HEAD_WIDTH), HEAD_WIDTH)
        for half in range(HALVES):
            out = outs[half * PEERS + peer]
            own = pl.ds(pl.multiple_of(heads + half * HALF, HALF), HALF)
            out[:, :HALF] = q_ref[0, :, own]
            out[:, HALF : 2 * HALF] = g_ref[0, :, own]
        out = outs[peer]
        out[:, 2 * HALF : 2 * HALF + HEAD_WIDTH] = k_ref[0, :, shared]
        out[:, 2 * HALF + HEAD_WIDTH :] = v_ref[0, :, shared]


def outgoing(place, queries, out_grad, dialogue_keys, dialogue_values):
    first = jax.ShapeDtypeStruct((OWN_ROWS, 2 * HALF + 2 * HEAD_WIDTH), bf16)
    second = jax.ShapeDtypeStruct((OWN_ROWS, 2 * HALF), bf16)
    outs = pl.pallas_call(
        outgoing_kernel,
        in_specs=[SMEM] + [pl.BlockSpec(memory_space=pltpu.HBM)] * 4,
        out_specs=[VMEM] * (2 * PEERS),
        out_shape=[first] * PEERS + [second] * PEERS,
        scratch_shapes=[
            pltpu.VMEM(x.shape, bf16) for x in (queries, out_grad, dialogue_keys, dialogue_values)
        ]
        + [pltpu.SemaphoreType.DMA((4,))],
        compiler_params=pltpu.CompilerParams(vmem_limit_bytes=60 * 1024 * 1024),
        cost_estimate=pl.CostEstimate(flops=0, bytes_accessed=5 * 10**6, transcendentals=0),
    )(place, queries, out_grad, dialogue_keys, dialogue_values)
    return outs[:PEERS], outs[PEERS:]


def assemble_kernel(place_ref, *refs):
    first, second = refs[:PEERS], refs[PEERS : 2 * PEERS]
    c_in, m_in, v_in, q_ref, k_ref, v_ref, c_out, m_out, v_out = refs[2 * PEERS :]
    c_out[...] = c_in[...]
    m_out[...] = BETA_ONE * m_in[...]
    v_out[...] = BETA_TWO * v_in[...]
    place = place_ref[0]
    for peer in range(PEERS):
        heads = part_start(place, peer, GROUP * HEAD_WIDTH)
        shared = pl.ds(part_start(place, peer, HEAD_WIDTH), HEAD_WIDTH)
        q_ref[0, :, pl.ds(heads, HALF)] = first[peer][...]
        q_ref[0, :, pl.ds(pl.multiple_of(heads + HALF, HALF), HALF)] = second[peer][:, :HALF]
        k_ref[0, :, shared] = second[peer][:, HALF : HALF + HEAD_WIDTH]
        v_ref[0, :, shared] = second[peer][:, HALF + HEAD_WIDTH :]


def assemble(place, first, second, trained):
    held = [jax.ShapeDtypeStruct(x.shape, f32) for x in trained]
    narrow = jax.ShapeDtypeStruct((1, OWN_ROWS, KEY_VALUE_HEADS * HEAD_WIDTH), bf16)
    return pl.pallas_call(
        assemble_kernel,
        in_specs=[SMEM] + [VMEM] * (2 * PEERS + 3),
        out_specs=[VMEM] * 6,
        out_shape=[jax.ShapeDtypeStruct((1, OWN_ROWS, QUERY_HEADS * HEAD_WIDTH), bf16), narrow, narrow, *held],
        compiler_params=PARAMS,
        cost_estimate=pl.CostEstimate(flops=0, bytes_accessed=3 * 10**6, transcendentals=0),
    )(place, *first, *second, *trained)


class Unit:
    def __init__(self, slot):
        self.slot = slot
        self.first = slot * ROWS
        self.rows = slice(self.first, self.first + ROWS)
        end = PREFIX_TOKENS + self.first + ROWS
        self.spans = [slice(s, min(s + CHUNK, end)) for s in range(0, end, CHUNK)]
        self.tops, self.top, self.total = [], None, None


def head_columns(head):
    return slice(head * HEAD_WIDTH, (head + 1) * HEAD_WIDTH)


def attention_kernel(last, length_ref, place_ref, *refs):
    tokens, shared = refs[:PEERS], refs[PEERS : 2 * PEERS]
    refs = refs[2 * PEERS :]
    prefix_refs, refs = refs[:PLANES], refs[PLANES:]
    if last:
        (dkeys_in, dvalues_in), refs = refs[:2], refs[2:]
    outs, refs = refs[:PEERS], refs[PEERS:]
    (dkeys_out, dvalues_out) = (None, None) if last else refs[:2]
    pgrad_ref = refs[0] if last else None
    refs = refs[1:] if last else refs[2:]
    keys, values, keys_t, values_t, dkeys, dvalues, exps, q_all, g_all, qgrad_all = refs
    if not last:
        dkeys, dvalues = dkeys_out, dvalues_out
    length, place = length_ref[0], place_ref[0]

    for k in range(PLANES):
        plane = slice(k * PLANE * SHARE, (k + 1) * PLANE * SHARE)
        keys[plane] = prefix_refs[k][:, :HEAD_WIDTH]
        values[plane] = prefix_refs[k][:, HEAD_WIDTH:]
    for peer in range(PEERS):
        rows = pl.ds(part_start(place, peer, OWN_ROWS), OWN_ROWS)
        there = pl.ds(pl.multiple_of(PREFIX_TOKENS + part_start(place, peer, OWN_ROWS), OWN_ROWS), OWN_ROWS)
        keys[there] = shared[peer][:, 2 * HALF : 2 * HALF + HEAD_WIDTH]
        values[there] = shared[peer][:, 2 * HALF + HEAD_WIDTH :]
        q_all[rows] = tokens[peer][:, :HALF]
        g_all[rows] = tokens[peer][:, HALF : 2 * HALF]
    for start in range(0, ALL_TOKENS, 256):
        span = slice(start, start + 256)
        keys_t[:, span] = turned(keys[span]).astype(bf16)
        values_t[:, span] = turned(values[span]).astype(bf16)
    dkeys[...] = jnp.zeros_like(dkeys)
    dvalues[...] = jnp.zeros_like(dvalues)

    def prepare(u):
        row_index = u.first + lax.broadcasted_iota(jnp.int32, (ROWS, HEAD_WIDTH), 0)
        zero = jnp.zeros((), bf16)
        heads = [head_columns(h) for h in range(HALF_HEADS)]
        u.q = jnp.concatenate([q_all[u.rows, h] for h in heads], 0)
        u.g = jnp.concatenate([jnp.where(row_index < length, g_all[u.rows, h], zero) for h in heads], 0)
        u.q_t = turned(u.q).astype(bf16)
        u.g_wide = turned(u.g)
        u.g_t = u.g_wide.astype(bf16)

    def forward(u, i):
        span = u.spans[i]
        scores = nn(keys[span], u.q_t)
        masked = PREFIX_TOKENS + u.first
        if span.stop > masked:
            skip = max(span.start, masked) - span.start
            shape = (span.stop - span.start - skip, WIDE)
            key_pos = span.start + skip - PREFIX_TOKENS + lax.broadcasted_iota(jnp.int32, shape, 0)
            row_pos = u.first + jnp.bitwise_and(lax.broadcasted_iota(jnp.int32, shape, 1), ROWS - 1)
            tail = jnp.where(key_pos <= row_pos, scores[skip:], MASKED)
            scores = jnp.concatenate([scores[:skip], tail], 0) if skip else tail
        top = jnp.max(scores, axis=0, keepdims=True)
        top = top if u.top is None else jnp.maximum(top, u.top)
        e = jnp.exp2((scores - top) * LOG2_SCALE)
        exps[u.slot, span] = e
        total = jnp.sum(e, axis=0, keepdims=True)
        u.total = total if u.top is None else u.total * jnp.exp2((u.top - top) * LOG2_SCALE) + total
        u.top = top
        u.tops.append(top)

    def end_forward(u):
        inverse = 1.0 / u.total
        u.factors = [jnp.exp2((top - u.top) * LOG2_SCALE) * inverse for top in u.tops]
        u.attended = jnp.zeros((HEAD_WIDTH, WIDE), f32)
        u.qgrad = jnp.zeros((HEAD_WIDTH, WIDE), f32)

    def attend(u, i):
        span = u.spans[i]
        half = (exps[u.slot, span] * u.factors[i]).astype(bf16)
        u.attended = u.attended + nn(values_t[:, span], half)
        dvalues[span] += nn(half, u.g)

    def end_attend(u):
        u.row_dot = jnp.sum(u.g_wide * u.attended.astype(bf16).astype(f32), axis=0, keepdims=True)

    def backward(u, i):
        span = u.spans[i]
        weight_grad = nn(values[span], u.g_t)
        score_grad = (exps[u.slot, span] * u.factors[i] * (weight_grad - u.row_dot)).astype(bf16)
        u.qgrad = u.qgrad + nn(keys_t[:, span], score_grad)
        dkeys[span] += nn(score_grad, u.q)

    def end_backward(u):
        turned_back = (u.qgrad * SCALE).T.astype(bf16)
        for h in range(HALF_HEADS):
            qgrad_all[u.rows, head_columns(h)] = turned_back[h * ROWS : (h + 1) * ROWS]

    units = [Unit(slot) for slot in range(BLOCKS)]
    for u in units:
        prepare(u)
    stages = ((forward, end_forward), (attend, end_attend), (backward, end_backward))
    for t in range(len(units) + len(stages) - 1):
        live = [(units[t - s], *stages[s]) for s in range(len(stages)) if 0 <= t - s < len(units)]
        for i in range(max(len(u.spans) for u, _, _ in live)):
            for u, work, _ in live:
                if i < len(u.spans):
                    work(u, i)
        for u, _, end in live:
            end(u)

    for peer in range(PEERS):
        rows = pl.ds(part_start(place, peer, OWN_ROWS), OWN_ROWS)
        outs[peer][:, :HALF] = qgrad_all[rows]
        if last:
            there = pl.ds(pl.multiple_of(PREFIX_TOKENS + part_start(place, peer, OWN_ROWS), OWN_ROWS), OWN_ROWS)
            outs[peer][:, HALF : HALF + HEAD_WIDTH] = ((dkeys[there] + dkeys_in[there]) * SCALE).astype(bf16)
            outs[peer][:, HALF + HEAD_WIDTH :] = (dvalues[there] + dvalues_in[there]).astype(bf16)
    if last:
        for k in range(PLANE * PLANES):
            rows = slice(k * SHARE, (k + 1) * SHARE)
            there = jnp.bitwise_xor(place_ref[1], (k // PLANES % 4) * 4 + k // PLANE), k % PLANES
            pgrad_ref[there[0], there[1], :, :HEAD_WIDTH] = ((dkeys[rows] + dkeys_in[rows]) * SCALE).astype(bf16)
            pgrad_ref[there[0], there[1], :, HEAD_WIDTH:] = (dvalues[rows] + dvalues_in[rows]).astype(bf16)


def attention(length, place, tokens, shared, prefix, sums=None):
    last = sums is not None
    out = jax.ShapeDtypeStruct((OWN_ROWS, HALF + (2 * HEAD_WIDTH if last else 0)), bf16)
    running = jax.ShapeDtypeStruct((ALL_TOKENS, HEAD_WIDTH), f32)
    outs = [out] * PEERS
    outs += [jax.ShapeDtypeStruct((PLANE, PLANES, SHARE, 2 * HEAD_WIDTH), bf16)] if last else [running] * 2
    operands = (*tokens, *shared, *prefix, *(sums or ()))
    half = pltpu.VMEM((ALL_TOKENS, HEAD_WIDTH), bf16)
    half_t = pltpu.VMEM((HEAD_WIDTH, ALL_TOKENS), bf16)
    wide = pltpu.VMEM((ALL_TOKENS, HEAD_WIDTH), f32)
    every = pltpu.VMEM((SLOT_COUNT, HALF), bf16)
    small = pltpu.VMEM((8, HEAD_WIDTH), f32)
    total = wide if last else small
    return pl.pallas_call(
        functools.partial(attention_kernel, last),
        in_specs=[SMEM] * 2 + [VMEM] * len(operands),
        out_specs=[VMEM] * len(outs),
        out_shape=outs,
        scratch_shapes=[
            half, half, half_t, half_t, total, total,
            pltpu.VMEM((BLOCKS, ALL_TOKENS, WIDE), f32),
            every, every, every,
        ],
        compiler_params=PARAMS,
        cost_estimate=pl.CostEstimate(flops=5 * 10**9, bytes_accessed=5 * 10**6, transcendentals=3 * 10**6),
    )(length, place, *operands)


def shards(
    queries,
    dialogue_keys,
    dialogue_values,
    out_grad,
    lengths,
    cartridge,
    first_moment,
    second_moment,
):
    place = jnp.stack([lax.axis_index("tensor"), lax.axis_index("dp") % PLANE])

    def exchange(parts):
        return [
            lax.ppermute(part, "tensor", [(i, i ^ peer) for i in range(PEERS)]) if peer else part
            for peer, part in enumerate(parts)
        ]

    def across(parts, stride=PLANE):
        size = PLANE * PLANES
        return [
            lax.ppermute(part, "dp", [(i, i ^ (k * stride)) for i in range(size)]) if k else part
            for k, part in enumerate(parts)
        ]

    own_prefix = cartridge.astype(bf16).reshape(SHARE, 2 * HEAD_WIDTH)
    column = across([own_prefix] * 4)
    first, second = outgoing(place, queries, out_grad, dialogue_keys, dialogue_values)
    column, own_part = lax.optimization_barrier((column, first[0]))
    first = [own_part, *first[1:]]
    column = jnp.concatenate(column)
    plane = jnp.concatenate(across([column] * 4, 4))
    prefix = across([plane] * 4, 1)
    first = exchange(first)
    first, second = lax.optimization_barrier((first, second))
    second = exchange(second)

    *first_grad, key_sum, value_sum = attention(lengths, place, first, first, prefix)
    first_back = exchange(first_grad)
    *second_grad, prefix_part = attention(lengths, place, second, first, prefix, (key_sum, value_sum))

    arrived = lax.all_to_all(prefix_part, "dp", 0, 0, axis_index_groups=IN_PLANE)
    second_back = exchange(second_grad)
    plane_sum = jnp.sum(arrived.astype(f32), 0).astype(bf16)
    arrived = across([plane_sum[k] for k in range(PLANES)])
    prefix_grad = sum(part.astype(f32) for part in arrived).reshape(cartridge.shape)
    q_grad, key_grad, value_grad, cartridge, old_m, old_v = assemble(
        place, first_back, second_back, (cartridge, first_moment, second_moment)
    )

    new_m = old_m + (1.0 - BETA_ONE) * prefix_grad
    new_v = old_v + (1.0 - BETA_TWO) * prefix_grad * prefix_grad
    update = new_m / (1.0 - BETA_ONE**STEP) / (jnp.sqrt(new_v / (1.0 - BETA_TWO**STEP)) + ADAM_EPS)
    new_cartridge = cartridge - LEARN_RATE * update
    return (q_grad, key_grad, value_grad, new_cartridge, new_m, new_v)


def solution(mesh):
    tokens = P("dp", "tensor", None)
    trained = P("dp", None, "tensor")
    return jax.shard_map(
        shards,
        mesh=mesh,
        in_specs=(tokens, tokens, tokens, tokens, P("dp"), trained, trained, trained),
        out_specs=(tokens, tokens, tokens, trained, trained, trained),
        check_vma=False,
    )
```
